128 devices in a mesh: wide: 32 (over x, z_hi, y), narrow: 4 (over z_lo, core).
Axes of the slice: x: 4, y: 4, z: 4 (z_hi: 2, z_lo: 2; z = z_hi * 2 + z_lo), core: 2. Of those that a mesh axis runs over, the one named last changes fastest.
Arguments:
- ratio_field: float32 [1024, 1024, 128], P('narrow', 'wide'), may hold values from 0.3 to 3
- estimate: float32 [1024, 1024, 128], P('narrow', 'wide'), may hold values from 0.1 to 10
- psf_spectrum: float32 [1024, 1024, 128], P(None, ('wide', 'narrow')), may hold values from 0.05 to 1
Outputs:
- new_estimate: float32 [1024, 1024, 128], P('narrow', 'wide')
The draws below stay inside these ranges and needn't reach their ends.
All inputs are finite; a program needn't handle non-finite values.
Results may differ from the reference program's by a relative error of at most 0.00013.
Values sent between devices are 32-bit elements; how exact they have to be, the bound alone decides.
No kernel may reach another device: no remote copies, remote signals or barrier semaphores. Data moves between devices by JAX's collectives and lax.ppermute only.
A program may use at most 128 MiB of HBM per device.

```python
import math
import jax
import jax.numpy as jnp
from jax import lax

NX = 1024
NY = 1024
NZ = 128


def block_scale(own_key, dims, cuts, smallest, largest):
    level = 1.0
    for position, blocks in cuts:
        draws = jax.random.uniform(jax.random.fold_in(jax.random.fold_in(own_key, 6), position), (blocks,), jnp.float32, smallest / len(cuts), largest / len(cuts))
        level = level * jnp.repeat(jnp.exp(draws), dims[position] // blocks).reshape((-1,) + (1,) * (len(dims) - 1 - position))
    return level


def setup_inputs(seed: int = 0) -> dict:
    key_list = jax.random.split(jax.random.key(seed), 4)
    ratio_field = jnp.clip(jnp.exp(math.log(3.0) - 2.3025851 * jax.random.uniform(key_list[0], (NX, NY, NZ), jnp.float32) ** block_scale(key_list[0], (NX, NY, NZ), ((0, 4), (1, 32)), -0.2, 0.2)), 0.3, 3.0)
    estimate = jnp.clip(jnp.exp(math.log(10.0) - 4.6051702 * jax.random.uniform(key_list[1], (NX, NY, NZ), jnp.float32) ** block_scale(key_list[1], (NX, NY, NZ), ((0, 4), (1, 32)), -0.2, 0.2)), 0.1, 10.0)
    psf_spectrum = jnp.clip(0.05 + 0.95 * jax.random.uniform(key_list[2], (NX, NY, NZ), jnp.float32) ** block_scale(key_list[2], (NX, NY, NZ), ((1, 128),), -0.2, 0.2), 0.05, 1.0)
    return {"ratio_field": ratio_field, "estimate": estimate, "psf_spectrum": psf_spectrum}


def cosine_table(length):
    freq = lax.iota(jnp.float32, length)[:, None]
    cells = lax.iota(jnp.float32, length)[None, :]
    scale = jnp.where(freq == 0, jnp.sqrt(1.0 / length), jnp.sqrt(2.0 / length)).astype(jnp.float32)
    return scale * jnp.cos(jnp.pi * (cells + 0.5) * freq / length)

def reference(ratio_field, estimate, psf_spectrum):
    highest = lax.Precision.HIGHEST
    table_x = cosine_table(NX)
    table_y = cosine_table(NY)
    table_z = cosine_table(NZ)
    volume = jnp.einsum('xyz,cz->xyc', ratio_field, table_z, precision=highest)
    volume = jnp.einsum('xyz,by->xbz', volume, table_y, precision=highest)
    volume = jnp.einsum('xyz,ax->ayz', volume, table_x, precision=highest)
    volume = volume * psf_spectrum
    volume = jnp.einsum('ayz,ax->xyz', volume, table_x, precision=highest)
    volume = jnp.einsum('xbz,by->xyz', volume, table_y, precision=highest)
    volume = jnp.einsum('xyc,cz->xyz', volume, table_z, precision=highest)
    return estimate * volume
```

```python
import functools

import jax
import jax.numpy as jnp
import ml_dtypes
import numpy as np
from jax import lax
from jax.experimental import pallas as pl
from jax.experimental.pallas import tpu as pltpu
from jax.sharding import PartitionSpec as P

F32 = jnp.float32
BF16 = jnp.bfloat16
ALL = ("x", "zh", "y", "zl", "core")
LIMIT = 40 * 1024 * 1024


def cosine_table(length):
    freq = np.arange(length, dtype=np.float32)[:, None]
    cells = np.arange(length, dtype=np.float32)[None, :]
    angle = np.float32(np.pi) * (cells + np.float32(0.5)) * freq / np.float32(length)
    scale = np.where(freq == 0, np.sqrt(np.float32(1.0 / length)), np.sqrt(np.float32(2.0 / length)))
    return scale.astype(np.float32) * np.cos(angle.astype(np.float64)).astype(np.float32)


def halves(table):
    high = table.astype(ml_dtypes.bfloat16)
    low = (table - high.astype(np.float32)).astype(ml_dtypes.bfloat16)
    return high, low


def split(value):
    high = value.astype(BF16)
    return high, (value - high.astype(F32)).astype(BF16)


def dot3(a_high, a_low, b_high, b_low):
    dot = functools.partial(jnp.dot, preferred_element_type=F32)
    return dot(a_high, b_high) + dot(a_high, b_low) + dot(a_low, b_high)


def device_id(px, zr, py, core):
    zr = zr % 4
    return (((px * 2 + zr // 2) * 4 + py) * 2 + zr % 2) * 2 + core


def moves(step, flip):
    return [
        (device_id(px, zr, py, core), device_id(px, zr + step, py, core ^ flip))
        for px in range(4)
        for py in range(4)
        for zr in range(4)
        for core in range(2)
    ]


def y_forward_kernel(order, volume, high, low, *rest):
    outs, rows = rest[:4], rest[4]
    v_high, v_low = split(volume[...].reshape(1024, 256))
    rows[...] = dot3(high[...], low[...], v_high, v_low)
    for dest in range(4):
        for q in range(2):
            begin = pl.multiple_of(order[dest * 2 + q] * 128, 128)
            outs[dest][q, 0] = rows[pl.ds(begin, 128), :]


def y_forward(order, volume, high, low, slot):
    part = jax.ShapeDtypeStruct((2, 2, 128, 256), F32)
    whole = pl.BlockSpec((1024, 1024), lambda c: (0, 0))
    return pl.pallas_call(
        y_forward_kernel,
        grid=(2,),
        in_specs=[
            pl.BlockSpec(memory_space=pltpu.SMEM),
            pl.BlockSpec((32, 1, 32, 256), lambda c: (0, 2 * slot + c, 0, 0)),
            whole,
            whole,
        ],
        out_specs=[pl.BlockSpec((2, 1, 128, 256), lambda c: (0, c, 0, 0))] * 4,
        out_shape=[part] * 4,
        scratch_shapes=[pltpu.VMEM((1024, 256), F32)],
        compiler_params=pltpu.CompilerParams(vmem_limit_bytes=LIMIT),
        cost_estimate=pl.CostEstimate(flops=3 * 2**30, bytes_accessed=8 * 2**20, transcendentals=0),
        name="y_forward",
    )(order, volume, high, low)


def x_forward_kernel(order, *refs):
    parts, (high, low, out, v_high, v_low) = refs[:4], refs[4:]

    @pl.when(pl.program_id(0) == 0)
    def _():
        for k in range(4):
            v_high[k], v_low[k] = split(parts[k][...].reshape(512, 256))

    total = None
    for k in range(4):
        block = order[k]
        term = dot3(v_high[k], v_low[k], high[block], low[block])
        total = term if total is None else total + term
    out[...] = total.reshape(2, 2, 128, 256)


def x_forward(order, parts, high, low):
    table = pl.BlockSpec((4, 256, 256), lambda a: (0, 0, a))
    return pl.pallas_call(
        x_forward_kernel,
        grid=(4,),
        in_specs=[pl.BlockSpec(memory_space=pltpu.SMEM)]
        + [pl.BlockSpec((2, 2, 128, 256), lambda a: (0, 0, 0, 0))] * 4
        + [table, table],
        out_specs=pl.BlockSpec((2, 2, 128, 256), lambda a: (0, 0, 0, a)),
        out_shape=jax.ShapeDtypeStruct((2, 2, 128, 1024), F32),
        scratch_shapes=[pltpu.VMEM((4, 512, 256), BF16)] * 2,
        compiler_params=pltpu.CompilerParams(vmem_limit_bytes=LIMIT),
        cost_estimate=pl.CostEstimate(flops=3 * 2**30, bytes_accessed=8 * 2**20, transcendentals=0),
        name="x_forward",
    )(order, *parts, high, low)


def x_inverse_kernel(order, spectrum, psf, high, low, *rest):
    outs, (v_high, v_low) = rest[:4], rest[4:]
    step = pl.program_id(0)

    @pl.when(step == 0)
    def _():
        for q in range(2):
            for c in range(2):
                value = spectrum[q, c] * psf[:, 0, q, c].reshape(128, 1024)
                rows = pl.ds((q * 2 + c) * 128, 128)
                v_high[rows, :], v_low[rows, :] = split(value)

    result = dot3(v_high[...], v_low[...], high[0], low[0]).reshape(2, 2, 128, 256)
    for dest in range(4):

        @pl.when(step == dest)
        def _():
            outs[dest][...] = result


def x_inverse(order, spectrum, psf, high, low, slot):
    part = jax.ShapeDtypeStruct((2, 2, 128, 256), F32)
    table = pl.BlockSpec((1, 1024, 256), lambda d, order: (order[d], 0, 0))
    return pl.pallas_call(
        x_inverse_kernel,
        grid_spec=pltpu.PrefetchScalarGridSpec(
            num_scalar_prefetch=1,
            grid=(4,),
            in_specs=[
                pl.BlockSpec((2, 2, 128, 1024), lambda d, order: (0, 0, 0, 0)),
                pl.BlockSpec((16, 1, 2, 2, 8, 1024), lambda d, order: (0, slot, 0, 0, 0, 0)),
                table,
                table,
            ],
            out_specs=[pl.BlockSpec((2, 2, 128, 256), lambda d, order: (0, 0, 0, 0))] * 4,
            scratch_shapes=[pltpu.VMEM((512, 1024), BF16)] * 2,
        ),
        out_shape=[part] * 4,
        compiler_params=pltpu.CompilerParams(vmem_limit_bytes=LIMIT),
        cost_estimate=pl.CostEstimate(flops=3 * 2**30, bytes_accessed=10 * 2**20, transcendentals=0),
        name="x_inverse",
    )(order, spectrum, psf, high, low)


def y_inverse_kernel(order, *refs):
    parts, (high, low), (out, v_high, v_low) = refs[:4], refs[4:6], refs[-3:]
    for dest in range(4):
        for q in range(2):
            rows = pl.ds(pl.multiple_of(order[dest * 2 + q] * 128, 128), 128)
            v_high[rows, :], v_low[rows, :] = split(parts[dest][q, 0])
    result = dot3(high[...], low[...], v_high[...], v_low[...])
    out[...] = result.reshape(32, 1, 32, 256)


def y_inverse(order, parts, high, low, slot, into):
    whole = pl.BlockSpec((1024, 1024), lambda c: (0, 0))
    in_specs = [pl.BlockSpec(memory_space=pltpu.SMEM)]
    in_specs += [pl.BlockSpec((2, 1, 128, 256), lambda c: (0, c, 0, 0))] * 4
    in_specs += [whole, whole]
    args = [order, *parts, high, low]
    aliases = {}
    if into is not None:
        in_specs.append(pl.BlockSpec(memory_space=pl.ANY))
        args.append(into)
        aliases = {7: 0}
    return pl.pallas_call(
        y_inverse_kernel,
        grid=(2,),
        in_specs=in_specs,
        out_specs=pl.BlockSpec((32, 1, 32, 256), lambda c: (0, 2 * slot + c, 0, 0)),
        out_shape=jax.ShapeDtypeStruct((32, 4, 32, 256), F32),
        scratch_shapes=[pltpu.VMEM((1024, 256), BF16)] * 2,
        input_output_aliases=aliases,
        compiler_params=pltpu.CompilerParams(vmem_limit_bytes=LIMIT),
        cost_estimate=pl.CostEstimate(flops=3 * 2**30, bytes_accessed=8 * 2**20, transcendentals=0),
        name="y_inverse",
    )(*args)


def local(ratio_field, estimate, psf_spectrum):
    px, zh, py, zl, core = (lax.axis_index(name) for name in ALL)
    ring = 2 * zh + zl
    narrow = 2 * zl + core

    cz = cosine_table(128)
    cz_order = np.array(
        [
            [
                (gx * 4 + gy) * 8 + ((2 * h + low - 1 + side) % 4) * 2 + i
                for gx in range(4)
                for h in range(2)
                for gy in range(4)
                for side in range(2)
                for i in range(2)
            ]
            for low in range(2)
        ]
    )
    table_z = jnp.asarray(cz[cz_order])[zl]
    pick_order = np.array(
        [
            [
                g * 8 + ((r + shift) % 4) * 2 + i
                for shift in (-1, 0, -2, 1)
                for g in range(16)
                for i in range(2)
            ]
            for r in range(4)
        ]
    )
    pick = jnp.asarray(np.eye(128, dtype=np.float32)[pick_order])[ring]
    cy = cosine_table(1024)
    b_order = np.array(
        [
            (((gx * 2 + r // 2) * 4 + gy) * 2 + r % 2) * 16 + k * 8 + j
            for r in range(4)
            for k in range(2)
            for gx in range(4)
            for gy in range(4)
            for j in range(8)
        ]
    )
    y_rows = [jnp.asarray(h) for h in halves(cy[b_order])]
    y_columns = [jnp.asarray(h) for h in halves(np.ascontiguousarray(cy[b_order].T))]
    cx = cosine_table(1024)
    x_rows = [jnp.asarray(h) for h in halves(np.ascontiguousarray(cx.T).reshape(4, 256, 1024))]
    x_columns = [
        jnp.asarray(h) for h in halves(np.ascontiguousarray(cx.reshape(1024, 4, 256).transpose(1, 0, 2)))
    ]

    b_sets = []
    for sign in (-1, 1):
        sets = []
        for near, flip in ((0, 0), (0, 1), (1, 0), (1, 1)):
            for q in range(2):
                place = ring + sign * (1 + q) if near else ring - sign * q
                sets.append((place % 4) * 2 + (core ^ flip))
        b_sets.append(jnp.stack(sets).astype(jnp.int32))
    x_blocks = jnp.stack([narrow ^ d for d in range(4)]).astype(jnp.int32)

    def exchange(lower, upper):
        send = functools.partial(lax.ppermute, axis_name=ALL)
        got_lower = [
            lower[0],
            send(lower[1], perm=moves(0, 1)),
            send(upper[2], perm=moves(1, 0)),
            send(upper[3], perm=moves(1, 1)),
        ]
        got_upper = [
            upper[0],
            send(upper[1], perm=moves(0, 1)),
            send(lower[2], perm=moves(-1, 0)),
            send(lower[3], perm=moves(-1, 1)),
        ]
        return got_lower, got_upper

    volume = jnp.einsum("xyz,cz->cyx", ratio_field, table_z, precision=lax.Precision.HIGH)
    volume = lax.all_to_all(volume, ("x", "zh", "y"), split_axis=0, concat_axis=0, tiled=True)
    volume = volume.reshape(32, 4, 32, 256)

    psf = jnp.einsum("abc,dc->dba", psf_spectrum, pick, precision=lax.Precision.HIGH)
    psf = psf.reshape(4, 16, 2, 8, 1024)
    from_above = lax.ppermute(psf[2], ALL, moves(-1, 0))
    from_below = lax.ppermute(psf[3], ALL, moves(1, 0))
    psf = jnp.stack([jnp.stack([psf[0], from_above], 1), jnp.stack([psf[1], from_below], 1)], 1)
    psf = lax.all_to_all(psf, ("x", "y"), split_axis=0, concat_axis=0, tiled=True)

    lower = y_forward(b_sets[0], volume, *y_rows, 0)
    upper = y_forward(b_sets[1], volume, *y_rows, 1)
    lower, upper = exchange(lower, upper)
    lower = x_forward(x_blocks, lower, *x_rows)
    upper = x_forward(x_blocks, upper, *x_rows)
    lower = x_inverse(x_blocks, lower, psf, *x_columns, 0)
    upper = x_inverse(x_blocks, upper, psf, *x_columns, 1)
    lower, upper = exchange(lower, upper)
    volume = y_inverse(b_sets[0], lower, *y_columns, 0, None)
    volume = y_inverse(b_sets[1], upper, *y_columns, 1, volume)

    volume = volume.reshape(128, 32, 256)
    volume = lax.all_to_all(volume, ("x", "zh", "y"), split_axis=0, concat_axis=0, tiled=True)
    volume = jnp.einsum("cyx,cz->xyz", volume, table_z, precision=lax.Precision.HIGH)
    return estimate * volume


def solution(mesh):
    cut = jax.sharding.Mesh(mesh.devices.reshape(4, 2, 4, 2, 2), ALL)
    wide, narrow = ("x", "zh", "y"), ("zl", "core")
    placed = (P(narrow, wide, None), P(narrow, wide, None), P(None, wide + narrow, None))
    return jax.shard_map(
        local, mesh=cut, in_specs=placed, out_specs=P(narrow, wide, None), check_vma=False
    )
```

```python
import functools

import jax
import jax.numpy as jnp
import ml_dtypes
import numpy as np
from jax import lax
from jax.experimental import pallas as pl
from jax.experimental.pallas import tpu as pltpu
from jax.sharding import PartitionSpec as P

F32 = jnp.float32
BF16 = jnp.bfloat16
ALL = ("x", "zh", "y", "zl", "core")
LIMIT = 12 * 1024 * 1024
EDGE_LIMIT = 57 * 1024 * 1024
FAR_LIMIT = 57 * 1024 * 1024
X_LIMIT = 48 * 1024 * 1024


def cosine_table(length):
    freq = np.arange(length, dtype=np.float32)[:, None]
    cells = np.arange(length, dtype=np.float32)[None, :]
    angle = np.float32(np.pi) * (cells + np.float32(0.5)) * freq / np.float32(length)
    scale = np.where(freq == 0, np.sqrt(np.float32(1.0 / length)), np.sqrt(np.float32(2.0 / length)))
    return scale.astype(np.float32) * np.cos(angle.astype(np.float64)).astype(np.float32)


def halves(table):
    high = table.astype(ml_dtypes.bfloat16)
    low = (table - high.astype(np.float32)).astype(ml_dtypes.bfloat16)
    return high, low


def split(value):
    high = value.astype(BF16)
    return high, (value - high.astype(F32)).astype(BF16)


def dot3(a_high, a_low, b_high, b_low):
    dot = functools.partial(jnp.dot, preferred_element_type=F32)
    return dot(a_high, b_high) + dot(a_high, b_low) + dot(a_low, b_high)


def device_id(px, zr, py, core):
    zr = zr % 4
    return (((px * 2 + zr // 2) * 4 + py) * 2 + zr % 2) * 2 + core


def moves(step, flip):
    return [
        (device_id(px, zr, py, core), device_id(px, zr + step, py, core ^ flip))
        for px in range(4)
        for py in range(4)
        for zr in range(4)
        for core in range(2)
    ]


VMEM = pl.BlockSpec(memory_space=pltpu.VMEM)
SMEM = pl.BlockSpec(memory_space=pltpu.SMEM)
PART = jax.ShapeDtypeStruct((2, 2, 128, 256), F32)
RING, X_BLOCKS, B_SETS = 0, 1, (5, 13)


def cost(flops, mib):
    return pl.CostEstimate(flops=int(flops), bytes_accessed=int(mib * 2**20), transcendentals=0)


def z_forward_kernel(_, volume, high, low, out):
    dot = functools.partial(jnp.dot, preferred_element_type=F32)
    for y in range(8):
        v_high, v_low = split(volume[:, y, :].T)
        out[:, y, :] = dot(high[0], v_high) + dot(high[0], v_low) + dot(low[0], v_high)


def z_forward(which, volume, high, low):
    table = pl.BlockSpec((1, 128, 128), lambda y, which: (which[0], 0, 0))
    return pl.pallas_call(
        z_forward_kernel,
        grid_spec=pltpu.PrefetchScalarGridSpec(
            num_scalar_prefetch=1,
            grid=(4,),
            in_specs=[pl.BlockSpec((256, 8, 128), lambda y, which: (0, y, 0)), table, table],
            out_specs=pl.BlockSpec((128, 8, 256), lambda y, which: (0, y, 0)),
        ),
        out_shape=jax.ShapeDtypeStruct((128, 32, 256), F32),
        compiler_params=pltpu.CompilerParams(vmem_limit_bytes=EDGE_LIMIT),
        cost_estimate=cost(3 * 2**28, 8),
        name="z_forward",
    )(which, volume, high, low)


def psf_forward_kernel(_, psf, pick, own, *far):
    dot = functools.partial(jnp.dot, preferred_element_type=F32)
    for b in range(8):
        v_high, v_low = split(psf[:, b, :].T)
        result = dot(pick[0], v_high) + dot(pick[0], v_low)
        result = result.reshape(4, 16, 2, 256)
        for kind in range(2):
            own[:, kind, 0, :, b, :] = result[kind]
            far[kind][:, :, b, :] = result[2 + kind]


def psf_forward(which, psf, pick):
    part = jax.ShapeDtypeStruct((16, 2, 8, 1024), F32)
    whole = jax.ShapeDtypeStruct((16, 2, 2, 2, 8, 1024), F32)
    return pl.pallas_call(
        psf_forward_kernel,
        grid_spec=pltpu.PrefetchScalarGridSpec(
            num_scalar_prefetch=1,
            grid=(4,),
            in_specs=[
                pl.BlockSpec((256, 8, 128), lambda a, which: (a, 0, 0)),
                pl.BlockSpec((1, 128, 128), lambda a, which: (which[0], 0, 0)),
            ],
            out_specs=[pl.BlockSpec((16, 2, 1, 2, 8, 256), lambda a, which: (0, 0, 0, 0, 0, a))]
            + [pl.BlockSpec((16, 2, 8, 256), lambda a, which: (0, 0, 0, a))] * 2,
        ),
        out_shape=[whole, part, part],
        compiler_params=pltpu.CompilerParams(vmem_limit_bytes=EDGE_LIMIT),
        cost_estimate=cost(2**29, 8),
        name="psf_forward",
    )(which, psf, pick)


def z_inverse_kernel(_, volume, estimate, high, low, out):
    dot = functools.partial(jnp.dot, preferred_element_type=F32)
    first = pl.program_id(0) * 8
    for y in range(8):
        v_high, v_low = split(volume[:, first + y, :].T)
        result = dot(v_high, high[0]) + dot(v_low, high[0]) + dot(v_high, low[0])
        out[:, y, :] = result * estimate[:, y, :]


def z_inverse(which, volume, estimate, high, low):
    rows = pl.BlockSpec((256, 8, 128), lambda y, which: (0, y, 0))
    table = pl.BlockSpec((1, 128, 128), lambda y, which: (which[0], 0, 0))
    return pl.pallas_call(
        z_inverse_kernel,
        grid_spec=pltpu.PrefetchScalarGridSpec(
            num_scalar_prefetch=1,
            grid=(4,),
            in_specs=[VMEM, rows, table, table],
            out_specs=rows,
        ),
        out_shape=jax.ShapeDtypeStruct((256, 32, 128), F32),
        compiler_params=pltpu.CompilerParams(vmem_limit_bytes=LIMIT),
        cost_estimate=cost(3 * 2**28, 12),
        name="z_inverse",
    )(which, volume, estimate, high, low)


def y_forward_kernel(slot, places, volume, high, low, *rest):
    outs, rows = rest[:4], rest[4]
    v_high, v_low = split(volume[...].reshape(1024, 256))
    rows[...] = dot3(high[...], low[...], v_high, v_low)
    for part in range(4):
        for q in range(2):
            begin = pl.multiple_of(places[B_SETS[slot] + part * 2 + q] * 128, 128)
            outs[part][q, 0] = rows[pl.ds(begin, 128), :]


def y_forward(places, volume, high, low, slot):
    whole = pl.BlockSpec((1024, 1024), lambda c: (0, 0))
    return pl.pallas_call(
        functools.partial(y_forward_kernel, slot),
        grid=(2,),
        in_specs=[
            SMEM,
            pl.BlockSpec((32, 1, 32, 256), lambda c: (0, 2 * slot + c, 0, 0)),
            whole,
            whole,
        ],
        out_specs=[pl.BlockSpec((2, 1, 128, 256), lambda c: (0, c, 0, 0))] * 4,
        out_shape=[PART] * 4,
        scratch_shapes=[pltpu.VMEM((1024, 256), F32)],
        compiler_params=pltpu.CompilerParams(vmem_limit_bytes=EDGE_LIMIT),
        cost_estimate=cost(3 * 2**30, 8),
        name="y_forward",
    )(places, volume, high, low)


def x_forward_kernel(places, *refs):
    parts, (high, low, out, v_high, v_low) = refs[:4], refs[4:]
    step = pl.program_id(0)

    @pl.when(step == 0)
    def _():
        for k in range(4):
            lanes = pl.ds(pl.multiple_of(places[X_BLOCKS + k] * 256, 256), 256)
            v_high[:, lanes], v_low[:, lanes] = split(parts[k][...].reshape(512, 256))

    total = dot3(v_high[...], v_low[...], high[...], low[...])
    out[...] = total.reshape(2, 2, 128, 256)


def x_forward(places, parts, high, low):
    return pl.pallas_call(
        x_forward_kernel,
        grid=(4,),
        in_specs=[SMEM]
        + [pl.BlockSpec((2, 2, 128, 256), lambda a: (0, 0, 0, 0))] * 4
        + [pl.BlockSpec((1024, 256), lambda a: (0, a))] * 2,
        out_specs=pl.BlockSpec((2, 2, 128, 256), lambda a: (0, 0, 0, a)),
        out_shape=jax.ShapeDtypeStruct((2, 2, 128, 1024), F32),
        scratch_shapes=[pltpu.VMEM((512, 1024), BF16)] * 2,
        compiler_params=pltpu.CompilerParams(vmem_limit_bytes=EDGE_LIMIT),
        cost_estimate=cost(3 * 2**30, 8),
        name="x_forward",
    )(places, *parts, high, low)


def x_inverse_kernel(slot, _, spectrum, psf, high, low, *rest):
    outs, (v_high, v_low) = rest[:4], rest[4:]
    step = pl.program_id(0)

    @pl.when(step == 0)
    def _():
        for q in range(2):
            for c in range(2):
                value = spectrum[q, c] * psf[:, slot, q, c].reshape(128, 1024)
                rows = pl.ds((q * 2 + c) * 128, 128)
                v_high[rows, :], v_low[rows, :] = split(value)

    result = dot3(v_high[...], v_low[...], high[0], low[0]).reshape(2, 2, 128, 256)
    for part in range(4):

        @pl.when(step == part)
        def _():
            outs[part][...] = result


def x_inverse(places, spectrum, psf, high, low, slot):
    table = pl.BlockSpec(
        (1, 1024, 256), lambda step, places: (places[X_BLOCKS + step], 0, 0)
    )
    return pl.pallas_call(
        functools.partial(x_inverse_kernel, slot),
        grid_spec=pltpu.PrefetchScalarGridSpec(
            num_scalar_prefetch=1,
            grid=(4,),
            in_specs=[
                pl.BlockSpec((2, 2, 128, 1024), lambda step, places: (0, 0, 0, 0)),
                VMEM,
                table,
                table,
            ],
            out_specs=[VMEM] * 4,
            scratch_shapes=[pltpu.VMEM((512, 1024), BF16)] * 2,
        ),
        out_shape=[PART] * 4,
        compiler_params=pltpu.CompilerParams(vmem_limit_bytes=X_LIMIT),
        cost_estimate=cost(3 * 2**30, 10),
        name="x_inverse",
    )(places, spectrum, psf, high, low)


def y_inverse_kernel(slot, places, *refs):
    parts, (high, low), (out, v_high, v_low) = refs[:4], refs[4:6], refs[-3:]
    c = pl.program_id(0)
    for part in range(4):
        for q in range(2):
            begin = places[B_SETS[slot] + part * 2 + q] * 128
            rows = pl.ds(pl.multiple_of(begin, 128), 128)
            v_high[rows, :], v_low[rows, :] = split(parts[part][q, c])
    result = dot3(high[...], low[...], v_high[...], v_low[...])
    out[:, 2 * slot + c] = result.reshape(32, 32, 256)


def y_inverse(places, parts, high, low, slot, into):
    args = [places, *parts, high, low] + ([] if into is None else [into])
    return pl.pallas_call(
        functools.partial(y_inverse_kernel, slot),
        grid=(2,),
        in_specs=[SMEM] + [VMEM] * (len(args) - 1),
        out_specs=VMEM,
        out_shape=jax.ShapeDtypeStruct((32, 4, 32, 256), F32),
        scratch_shapes=[pltpu.VMEM((1024, 256), BF16)] * 2,
        input_output_aliases={} if into is None else {7: 0},
        compiler_params=pltpu.CompilerParams(vmem_limit_bytes=LIMIT),
        cost_estimate=cost(3 * 2**30, 8),
        name="y_inverse",
    )(*args)


def local(ratio_field, estimate, psf_spectrum):
    px, zh, py, zl, core = (lax.axis_index(name) for name in ALL)
    ring = 2 * zh + zl
    narrow = 2 * zl + core

    cz = cosine_table(128)
    cz_order = np.array(
        [
            [
                (gx * 4 + gy) * 8 + ((2 * h + low - 1 + side) % 4) * 2 + i
                for gx in range(4)
                for h in range(2)
                for gy in range(4)
                for side in range(2)
                for i in range(2)
            ]
            for low in range(2)
        ]
    )
    z_rows = [jnp.asarray(h) for h in halves(cz[cz_order])]
    pick_order = np.array(
        [
            [
                g * 8 + ((r + shift) % 4) * 2 + i
                for shift in (-1, 0, -2, 1)
                for g in range(16)
                for i in range(2)
            ]
            for r in range(4)
        ]
    )
    pick = jnp.asarray(np.eye(128, dtype=np.float32)[pick_order].astype(ml_dtypes.bfloat16))
    cy = cosine_table(1024)
    b_order = np.array(
        [
            (((gx * 2 + r // 2) * 4 + gy) * 2 + r % 2) * 16 + k * 8 + j
            for r in range(4)
            for k in range(2)
            for gx in range(4)
            for gy in range(4)
            for j in range(8)
        ]
    )
    y_rows = [jnp.asarray(h) for h in halves(cy[b_order])]
    y_columns = [jnp.asarray(h) for h in halves(np.ascontiguousarray(cy[b_order].T))]
    cx = cosine_table(1024)
    x_rows = [jnp.asarray(h) for h in halves(np.ascontiguousarray(cx.T))]
    x_columns = [
        jnp.asarray(h) for h in halves(np.ascontiguousarray(cx.reshape(1024, 4, 256).transpose(1, 0, 2)))
    ]

    partners = ((0, 0), (0, 1), (1, 0), (1, 1))
    places = [ring] + [narrow ^ (2 * far + flip) for far, flip in partners]
    for sign in (-1, 1):
        for far, flip in partners:
            for q in range(2):
                place = ring + sign * (1 + q) if far else ring - sign * q
                places.append((place % 4) * 2 + (core ^ flip))
    places = jnp.stack(places).astype(jnp.int32)

    def send(value, step, flip):
        return lax.ppermute(value, ALL, moves(step, flip))

    def first_all_to_all(value, axes):
        return lax.all_to_all(value, axes, split_axis=0, concat_axis=0, tiled=True)

    def one(value):
        return jnp.asarray(value, jnp.int32).reshape(1)

    def after(value, done):
        return lax.optimization_barrier((value, done))[0]

    volume = z_forward(one(zl), ratio_field, *z_rows)
    volume = first_all_to_all(volume, ("x", "zh", "y")).reshape(32, 4, 32, 256)

    psf, up, down = psf_forward(places, psf_spectrum, pick)
    above, below = send(up, -1, 0), send(down, 1, 0)
    psf, above, below = after((psf, above, below), volume)
    psf = psf.at[:, 0, 1].set(above).at[:, 1, 1].set(below)
    psf = first_all_to_all(psf, ("x", "y"))

    def exchange(lower, upper):
        got_lower = [lower[0], send(lower[1], 0, 1), send(upper[2], 1, 0), send(upper[3], 1, 1)]
        got_upper = [upper[0], send(upper[1], 0, 1), send(lower[2], -1, 0), send(lower[3], -1, 1)]
        return got_lower, got_upper

    lower = y_forward(places, volume, *y_rows, 0)
    upper = y_forward(places, volume, *y_rows, 1)
    lower, upper = exchange(lower, upper)
    lower = x_forward(places, lower, *x_rows)
    upper = x_forward(places, upper, *x_rows)

    lower = x_inverse(places, lower, psf, *x_columns, 0)
    upper = x_inverse(places, upper, psf, *x_columns, 1)
    lower, upper = exchange(lower, upper)
    volume = y_inverse(places, upper, *y_columns, 1, None)
    volume = y_inverse(places, lower, *y_columns, 0, volume)

    volume = first_all_to_all(volume.reshape(128, 32, 256), ("x", "zh", "y"))
    return z_inverse(one(zl), volume, estimate, *z_rows)


def solution(mesh):
    cut = jax.sharding.Mesh(mesh.devices.reshape(4, 2, 4, 2, 2), ALL)
    wide, narrow = ("x", "zh", "y"), ("zl", "core")
    placed = (P(narrow, wide, None), P(narrow, wide, None), P(None, wide + narrow, None))
    return jax.shard_map(
        local, mesh=cut, in_specs=placed, out_specs=P(narrow, wide, None), check_vma=False
    )
```

```python
import functools

import jax
import jax.numpy as jnp
import ml_dtypes
import numpy as np
from jax import lax
from jax.experimental import pallas as pl
from jax.experimental.pallas import tpu as pltpu
from jax.sharding import PartitionSpec as P

F32 = jnp.float32
BF16 = jnp.bfloat16
ALL = ("x", "zh", "y", "zl", "core")
LIMIT = 12 * 1024 * 1024
EDGE_LIMIT = 57 * 1024 * 1024
FAR_LIMIT = 57 * 1024 * 1024
X_LIMIT = 50 * 1024 * 1024


def cosine_table(length):
    freq = np.arange(length, dtype=np.float32)[:, None]
    cells = np.arange(length, dtype=np.float32)[None, :]
    angle = np.float32(np.pi) * (cells + np.float32(0.5)) * freq / np.float32(length)
    scale = np.where(freq == 0, np.sqrt(np.float32(1.0 / length)), np.sqrt(np.float32(2.0 / length)))
    return scale.astype(np.float32) * np.cos(angle.astype(np.float64)).astype(np.float32)


def halves(table):
    high = table.astype(ml_dtypes.bfloat16)
    low = (table - high.astype(np.float32)).astype(ml_dtypes.bfloat16)
    return high, low


def split(value):
    high = value.astype(BF16)
    return high, (value - high.astype(F32)).astype(BF16)


def dot3(a_high, a_low, b_high, b_low):
    dot = functools.partial(jnp.dot, preferred_element_type=F32)
    return dot(a_high, b_high) + dot(a_high, b_low) + dot(a_low, b_high)


def device_id(px, zr, py, core):
    zr = zr % 4
    return (((px * 2 + zr // 2) * 4 + py) * 2 + zr % 2) * 2 + core


def moves(step, flip):
    return [
        (device_id(px, zr, py, core), device_id(px, zr + step, py, core ^ flip))
        for px in range(4)
        for py in range(4)
        for zr in range(4)
        for core in range(2)
    ]


VMEM = pl.BlockSpec(memory_space=pltpu.VMEM)
SMEM = pl.BlockSpec(memory_space=pltpu.SMEM)
PART = jax.ShapeDtypeStruct((2, 2, 128, 256), F32)
RING, X_BLOCKS, B_SETS = 0, 1, 5
BOTH = jax.ShapeDtypeStruct((2, 2, 2, 128, 256), F32)


def cost(flops, mib):
    return pl.CostEstimate(flops=int(flops), bytes_accessed=int(mib * 2**20), transcendentals=0)


def z_forward_kernel(_, volume, high, low, out):
    dot = functools.partial(jnp.dot, preferred_element_type=F32)
    for y in range(8):
        v_high, v_low = split(volume[:, y, :].T)
        out[:, y, :] = dot(high[0], v_high) + dot(high[0], v_low) + dot(low[0], v_high)


def z_forward(which, volume, high, low):
    table = pl.BlockSpec((1, 128, 128), lambda y, which: (which[0], 0, 0))
    return pl.pallas_call(
        z_forward_kernel,
        grid_spec=pltpu.PrefetchScalarGridSpec(
            num_scalar_prefetch=1,
            grid=(4,),
            in_specs=[pl.BlockSpec((256, 8, 128), lambda y, which: (0, y, 0)), table, table],
            out_specs=pl.BlockSpec((128, 8, 256), lambda y, which: (0, y, 0)),
        ),
        out_shape=jax.ShapeDtypeStruct((128, 32, 256), F32),
        compiler_params=pltpu.CompilerParams(vmem_limit_bytes=EDGE_LIMIT),
        cost_estimate=cost(3 * 2**28, 8),
        name="z_forward",
    )(which, volume, high, low)


def psf_forward_kernel(_, psf, pick, own, far):
    dot = functools.partial(jnp.dot, preferred_element_type=F32)
    for b in range(8):
        v_high, v_low = split(psf[:, b, :].T)
        result = dot(pick[0], v_high) + dot(pick[0], v_low)
        result = result.reshape(4, 16, 2, 256)
        for kind in range(2):
            own[:, kind, :, b, :] = result[kind]
            far[:, kind, :, b, :] = result[2 + kind]


def psf_forward(which, psf, pick):
    near = jax.ShapeDtypeStruct((16, 2, 2, 8, 1024), F32)
    return pl.pallas_call(
        psf_forward_kernel,
        grid_spec=pltpu.PrefetchScalarGridSpec(
            num_scalar_prefetch=1,
            grid=(4,),
            in_specs=[
                pl.BlockSpec((256, 8, 128), lambda a, which: (a, 0, 0)),
                pl.BlockSpec((1, 128, 128), lambda a, which: (which[0], 0, 0)),
            ],
            out_specs=[pl.BlockSpec((16, 2, 2, 8, 256), lambda a, which: (0, 0, 0, 0, a))] * 2,
        ),
        out_shape=[near, near],
        compiler_params=pltpu.CompilerParams(vmem_limit_bytes=EDGE_LIMIT),
        cost_estimate=cost(2**29, 8),
        name="psf_forward",
    )(which, psf, pick)


def z_inverse_kernel(_, volume, estimate, high, low, out):
    dot = functools.partial(jnp.dot, preferred_element_type=F32)
    first = pl.program_id(0) * 8
    for y in range(8):
        v_high, v_low = split(volume[:, first + y, :].T)
        result = dot(v_high, high[0]) + dot(v_low, high[0]) + dot(v_high, low[0])
        out[:, y, :] = result * estimate[:, y, :]


def z_inverse(which, volume, estimate, high, low):
    rows = pl.BlockSpec((256, 8, 128), lambda y, which: (0, y, 0))
    table = pl.BlockSpec((1, 128, 128), lambda y, which: (which[0], 0, 0))
    return pl.pallas_call(
        z_inverse_kernel,
        grid_spec=pltpu.PrefetchScalarGridSpec(
            num_scalar_prefetch=1,
            grid=(4,),
            in_specs=[VMEM, rows, table, table],
            out_specs=rows,
        ),
        out_shape=jax.ShapeDtypeStruct((256, 32, 128), F32),
        compiler_params=pltpu.CompilerParams(vmem_limit_bytes=LIMIT),
        cost_estimate=cost(3 * 2**28, 12),
        name="z_inverse",
    )(which, volume, estimate, high, low)


def y_forward_kernel(places, volume, high, low, own, across, *rest):
    along, rows = rest[:4], rest[4]
    slot = pl.program_id(0) // 2
    v_high, v_low = split(volume[...].reshape(1024, 256))
    rows[...] = dot3(high[...], low[...], v_high, v_low)

    def block(part, q):
        begin = places[B_SETS + slot * 8 + part * 2 + q] * 128
        return rows[pl.ds(pl.multiple_of(begin, 128), 128), :]

    for q in range(2):
        own[0, q, 0] = block(0, q)
        across[0, q, 0] = block(1, q)
        for side in range(2):

            @pl.when(slot == side)
            def _():
                along[2 * side][q, 0] = block(2, q)
                along[2 * side + 1][q, 0] = block(3, q)


def y_forward(places, volume, high, low):
    whole = pl.BlockSpec((1024, 1024), lambda c: (0, 0))
    both = pl.BlockSpec((1, 2, 1, 128, 256), lambda c: (c // 2, 0, c % 2, 0, 0))
    down = pl.BlockSpec((2, 1, 128, 256), lambda c: (0, jnp.minimum(c, 1), 0, 0))
    up = pl.BlockSpec((2, 1, 128, 256), lambda c: (0, jnp.maximum(c - 2, 0), 0, 0))
    return pl.pallas_call(
        y_forward_kernel,
        grid=(4,),
        in_specs=[SMEM, pl.BlockSpec((32, 1, 32, 256), lambda c: (0, c, 0, 0)), whole, whole],
        out_specs=[both, both, down, down, up, up],
        out_shape=[BOTH, BOTH] + [PART] * 4,
        scratch_shapes=[pltpu.VMEM((1024, 256), F32)],
        compiler_params=pltpu.CompilerParams(vmem_limit_bytes=EDGE_LIMIT),
        cost_estimate=cost(6 * 2**30, 12),
        name="y_forward",
    )(places, volume, high, low)


def x_forward_kernel(places, own, across, *refs):
    along, (high, low, out, v_high, v_low) = refs[:4], refs[4:]
    step = pl.program_id(0)

    @pl.when(step == 0)
    def _():
        for slot in range(2):
            for k in range(4):
                part = (own, across)[k].at[slot] if k < 2 else along[2 * slot + k - 2]
                rows = pl.ds(slot * 512, 512)
                lanes = pl.ds(pl.multiple_of(places[X_BLOCKS + k] * 256, 256), 256)
                v_high[rows, lanes], v_low[rows, lanes] = split(part[...].reshape(512, 256))

    total = dot3(v_high[...], v_low[...], high[...], low[...])
    out[...] = total.reshape(2, 2, 2, 128, 256)


def x_forward(places, own, across, along, high, low):
    return pl.pallas_call(
        x_forward_kernel,
        grid=(4,),
        in_specs=[SMEM]
        + [pl.BlockSpec((2, 2, 2, 128, 256), lambda a: (0, 0, 0, 0, 0))] * 2
        + [pl.BlockSpec((2, 2, 128, 256), lambda a: (0, 0, 0, 0))] * 4
        + [pl.BlockSpec((1024, 256), lambda a: (0, a))] * 2,
        out_specs=pl.BlockSpec((2, 2, 2, 128, 256), lambda a: (0, 0, 0, 0, a)),
        out_shape=jax.ShapeDtypeStruct((2, 2, 2, 128, 1024), F32),
        scratch_shapes=[pltpu.VMEM((1024, 1024), BF16)] * 2,
        compiler_params=pltpu.CompilerParams(vmem_limit_bytes=EDGE_LIMIT),
        cost_estimate=cost(6 * 2**30, 12),
        name="x_forward",
    )(places, own, across, *along, high, low)


def x_inverse_kernel(_, spectrum, near, above, below, high, low, own, across, *rest):
    along, (v_high, v_low) = rest[:4], rest[4:]
    step = pl.program_id(0)

    @pl.when(step == 0)
    def _():
        for slot in range(2):
            for q in range(2):
                for c in range(2):
                    psf = (above, below)[slot][:, c] if q else near[:, slot, c]
                    value = spectrum[slot, q, c] * psf.reshape(128, 1024)
                    rows = pl.ds(slot * 512 + q * 256 + c * 128, 128)
                    v_high[rows, :], v_low[rows, :] = split(value)

    result = dot3(v_high[...], v_low[...], high[0], low[0]).reshape(2, 2, 2, 128, 256)
    for k in range(2):

        @pl.when(step == k)
        def _():
            along[k][...] = result[0]
            along[2 + k][...] = result[1]

    @pl.when(step == 2)
    def _():
        across[...] = result

    @pl.when(step == 3)
    def _():
        own[...] = result


def x_inverse(places, spectrum, near, above, below, high, low):
    def block(step, places):
        return places[X_BLOCKS + jnp.where(step < 2, step + 2, 3 - step)], 0, 0

    table = pl.BlockSpec((1, 1024, 256), block)
    whole = pl.BlockSpec((2, 2, 2, 128, 1024), lambda step, places: (0, 0, 0, 0, 0))
    far = pl.BlockSpec((16, 2, 8, 1024), lambda step, places: (0, 0, 0, 0))
    return pl.pallas_call(
        x_inverse_kernel,
        grid_spec=pltpu.PrefetchScalarGridSpec(
            num_scalar_prefetch=1,
            grid=(4,),
            in_specs=[whole, VMEM, far, far, table, table],
            out_specs=[VMEM] * 6,
            scratch_shapes=[pltpu.VMEM((1024, 1024), BF16)] * 2,
        ),
        out_shape=[BOTH, BOTH] + [PART] * 4,
        compiler_params=pltpu.CompilerParams(vmem_limit_bytes=X_LIMIT),
        cost_estimate=cost(6 * 2**30, 16),
        name="x_inverse",
    )(places, spectrum, near, above, below, high, low)


def y_inverse_kernel(places, own, across, *refs):
    along, (high, low, out, v_high, v_low) = refs[:4], refs[4:]
    slot, c = pl.program_id(0) // 2, pl.program_id(0) % 2

    def place(part, q, value):
        begin = places[B_SETS + slot * 8 + part * 2 + q] * 128
        rows = pl.ds(pl.multiple_of(begin, 128), 128)
        v_high[rows, :], v_low[rows, :] = split(value)

    for q in range(2):
        place(0, q, own[slot, q, c])
        place(1, q, across[slot, q, c])
        for side in range(2):

            @pl.when(slot == side)
            def _():
                place(2, q, along[2 * side][q, c])
                place(3, q, along[2 * side + 1][q, c])

    result = dot3(high[...], low[...], v_high[...], v_low[...])
    out[:, 2 * slot + c] = result.reshape(32, 32, 256)


def y_inverse(places, own, across, along, high, low):
    return pl.pallas_call(
        y_inverse_kernel,
        grid=(4,),
        in_specs=[SMEM] + [VMEM] * 8,
        out_specs=VMEM,
        out_shape=jax.ShapeDtypeStruct((32, 4, 32, 256), F32),
        scratch_shapes=[pltpu.VMEM((1024, 256), BF16)] * 2,
        compiler_params=pltpu.CompilerParams(vmem_limit_bytes=LIMIT),
        cost_estimate=cost(6 * 2**30, 12),
        name="y_inverse",
    )(places, own, across, *along, high, low)


def local(ratio_field, estimate, psf_spectrum):
    px, zh, py, zl, core = (lax.axis_index(name) for name in ALL)
    ring = 2 * zh + zl
    narrow = 2 * zl + core

    cz = cosine_table(128)
    cz_order = np.array(
        [
            [
                (gx * 4 + gy) * 8 + ((2 * h + low - 1 + side) % 4) * 2 + i
                for gx in range(4)
                for h in range(2)
                for gy in range(4)
                for side in range(2)
                for i in range(2)
            ]
            for low in range(2)
        ]
    )
    z_rows = [jnp.asarray(h) for h in halves(cz[cz_order])]
    pick_order = np.array(
        [
            [
                g * 8 + ((r + shift) % 4) * 2 + i
                for shift in (-1, 0, -2, 1)
                for g in range(16)
                for i in range(2)
            ]
            for r in range(4)
        ]
    )
    pick = jnp.asarray(np.eye(128, dtype=np.float32)[pick_order].astype(ml_dtypes.bfloat16))
    cy = cosine_table(1024)
    b_order = np.array(
        [
            (((gx * 2 + r // 2) * 4 + gy) * 2 + r % 2) * 16 + k * 8 + j
            for r in range(4)
            for k in range(2)
            for gx in range(4)
            for gy in range(4)
            for j in range(8)
        ]
    )
    y_rows = [jnp.asarray(h) for h in halves(cy[b_order])]
    y_columns = [jnp.asarray(h) for h in halves(np.ascontiguousarray(cy[b_order].T))]
    cx = cosine_table(1024)
    x_rows = [jnp.asarray(h) for h in halves(np.ascontiguousarray(cx.T))]
    x_columns = [
        jnp.asarray(h) for h in halves(np.ascontiguousarray(cx.reshape(1024, 4, 256).transpose(1, 0, 2)))
    ]

    partners = ((0, 0), (0, 1), (1, 0), (1, 1))
    places = [ring] + [narrow ^ (2 * far + flip) for far, flip in partners]
    for sign in (-1, 1):
        for far, flip in partners:
            for q in range(2):
                place = ring + sign * (1 + q) if far else ring - sign * q
                places.append((place % 4) * 2 + (core ^ flip))
    places = jnp.stack(places).astype(jnp.int32)

    def send(value, step, flip):
        return lax.ppermute(value, ALL, moves(step, flip))

    def first_all_to_all(value, axes):
        return lax.all_to_all(value, axes, split_axis=0, concat_axis=0, tiled=True)

    def one(value):
        return jnp.asarray(value, jnp.int32).reshape(1)

    def after(value, done):
        return lax.optimization_barrier((value, done))[0]

    volume = z_forward(one(zl), ratio_field, *z_rows)
    volume = first_all_to_all(volume, ("x", "zh", "y")).reshape(32, 4, 32, 256)

    near, far = psf_forward(places, psf_spectrum, pick)
    far = first_all_to_all(after(far, volume), ("x", "y"))

    def exchange(own, across, *along):
        from_above = [send(along[0], -1, 0), send(along[1], -1, 1)]
        from_below = [send(along[2], 1, 0), send(along[3], 1, 1)]
        return own, send(across, 0, 1), from_below + from_above

    parts = exchange(*y_forward(places, volume, *y_rows))
    near = first_all_to_all(after(near, (far, parts[2][0], parts[2][2])), ("x", "y"))
    above, below = send(far[:, 0], -1, 0), send(far[:, 1], 1, 0)
    spectrum = x_forward(places, *parts, *x_rows)
    parts = exchange(*x_inverse(places, spectrum, near, above, below, *x_columns))
    volume = y_inverse(places, *parts, *y_columns)

    volume = first_all_to_all(volume.reshape(128, 32, 256), ("x", "zh", "y"))
    return z_inverse(one(zl), volume, estimate, *z_rows)


def solution(mesh):
    cut = jax.sharding.Mesh(mesh.devices.reshape(4, 2, 4, 2, 2), ALL)
    wide, narrow = ("x", "zh", "y"), ("zl", "core")
    placed = (P(narrow, wide, None), P(narrow, wide, None), P(None, wide + narrow, None))
    return jax.shard_map(
        local, mesh=cut, in_specs=placed, out_specs=P(narrow, wide, None), check_vma=False
    )
```

```python
import functools

import jax
import jax.numpy as jnp
import ml_dtypes
import numpy as np
from jax import lax
from jax.experimental import pallas as pl
from jax.experimental.pallas import tpu as pltpu
from jax.sharding import PartitionSpec as P

F32 = jnp.float32
BF16 = jnp.bfloat16
ALL = ("x", "zh", "y", "zl", "core")
LIMIT = 12 * 1024 * 1024
EDGE_LIMIT = 57 * 1024 * 1024
FAR_LIMIT = 57 * 1024 * 1024
X_LIMIT = 50 * 1024 * 1024


def cosine_table(length):
    freq = np.arange(length, dtype=np.float32)[:, None]
    cells = np.arange(length, dtype=np.float32)[None, :]
    angle = np.float32(np.pi) * (cells + np.float32(0.5)) * freq / np.float32(length)
    scale = np.where(freq == 0, np.sqrt(np.float32(1.0 / length)), np.sqrt(np.float32(2.0 / length)))
    return scale.astype(np.float32) * np.cos(angle.astype(np.float64)).astype(np.float32)


def halves(table):
    high = table.astype(ml_dtypes.bfloat16)
    low = (table - high.astype(np.float32)).astype(ml_dtypes.bfloat16)
    return high, low


def split(value):
    high = value.astype(BF16)
    return high, (value - high.astype(F32)).astype(BF16)


def dot3(a_high, a_low, b_high, b_low):
    dot = functools.partial(jnp.dot, preferred_element_type=F32)
    return dot(a_high, b_high) + dot(a_high, b_low) + dot(a_low, b_high)


def device_id(px, zr, py, core):
    zr = zr % 4
    return (((px * 2 + zr // 2) * 4 + py) * 2 + zr % 2) * 2 + core


def moves(step, flip):
    return [
        (device_id(px, zr, py, core), device_id(px, zr + step, py, core ^ flip))
        for px in range(4)
        for py in range(4)
        for zr in range(4)
        for core in range(2)
    ]


VMEM = pl.BlockSpec(memory_space=pltpu.VMEM)
SMEM = pl.BlockSpec(memory_space=pltpu.SMEM)
PART = jax.ShapeDtypeStruct((2, 2, 128, 256), F32)
RING, X_BLOCKS, B_SETS = 0, 1, 5
BOTH = jax.ShapeDtypeStruct((2, 2, 2, 128, 256), F32)


def cost(flops, mib):
    return pl.CostEstimate(flops=int(flops), bytes_accessed=int(mib * 2**20), transcendentals=0)


def z_forward_kernel(_, volume, high, low, out):
    dot = functools.partial(jnp.dot, preferred_element_type=F32)
    for y in range(8):
        v_high, v_low = split(volume[:, y, :].T)
        out[:, y, :] = dot(high[0], v_high) + dot(high[0], v_low) + dot(low[0], v_high)


def z_forward(which, volume, high, low):
    table = pl.BlockSpec((1, 128, 128), lambda y, which: (which[0], 0, 0))
    return pl.pallas_call(
        z_forward_kernel,
        grid_spec=pltpu.PrefetchScalarGridSpec(
            num_scalar_prefetch=1,
            grid=(4,),
            in_specs=[pl.BlockSpec((256, 8, 128), lambda y, which: (0, y, 0)), table, table],
            out_specs=pl.BlockSpec((128, 8, 256), lambda y, which: (0, y, 0)),
        ),
        out_shape=jax.ShapeDtypeStruct((128, 32, 256), F32),
        compiler_params=pltpu.CompilerParams(vmem_limit_bytes=EDGE_LIMIT),
        cost_estimate=cost(3 * 2**28, 8),
        name="z_forward",
    )(which, volume, high, low)


def psf_forward_kernel(_, psf, pick, own, far):
    dot = functools.partial(jnp.dot, preferred_element_type=F32)
    for b in range(8):
        v_high, v_low = split(psf[:, b, :].T)
        result = dot(pick[0], v_high) + dot(pick[0], v_low)
        result = result.reshape(4, 16, 2, 256)
        for kind in range(2):
            own[:, kind, :, b, :] = result[kind]
            far[:, kind, :, b, :] = result[2 + kind]


def psf_forward(which, psf, pick):
    near = jax.ShapeDtypeStruct((16, 2, 2, 8, 1024), F32)
    return pl.pallas_call(
        psf_forward_kernel,
        grid_spec=pltpu.PrefetchScalarGridSpec(
            num_scalar_prefetch=1,
            grid=(4,),
            in_specs=[
                pl.BlockSpec((256, 8, 128), lambda a, which: (a, 0, 0)),
                pl.BlockSpec((1, 128, 128), lambda a, which: (which[0], 0, 0)),
            ],
            out_specs=[pl.BlockSpec((16, 2, 2, 8, 256), lambda a, which: (0, 0, 0, 0, a))] * 2,
        ),
        out_shape=[near, near],
        compiler_params=pltpu.CompilerParams(vmem_limit_bytes=EDGE_LIMIT),
        cost_estimate=cost(2**29, 8),
        name="psf_forward",
    )(which, psf, pick)


def z_inverse_kernel(_, volume, estimate, high, low, out):
    dot = functools.partial(jnp.dot, preferred_element_type=F32)
    first = pl.program_id(0) * 8
    for y in range(8):
        v_high, v_low = split(volume[:, first + y, :].T)
        result = dot(v_high, high[0]) + dot(v_low, high[0]) + dot(v_high, low[0])
        out[:, y, :] = result * estimate[:, y, :]


def z_inverse(which, volume, estimate, high, low):
    rows = pl.BlockSpec((256, 8, 128), lambda y, which: (0, y, 0))
    table = pl.BlockSpec((1, 128, 128), lambda y, which: (which[0], 0, 0))
    return pl.pallas_call(
        z_inverse_kernel,
        grid_spec=pltpu.PrefetchScalarGridSpec(
            num_scalar_prefetch=1,
            grid=(4,),
            in_specs=[VMEM, rows, table, table],
            out_specs=rows,
        ),
        out_shape=jax.ShapeDtypeStruct((256, 32, 128), F32),
        compiler_params=pltpu.CompilerParams(vmem_limit_bytes=LIMIT),
        cost_estimate=cost(3 * 2**28, 12),
        name="z_inverse",
    )(which, volume, estimate, high, low)


def y_forward_kernel(places, volume, high, low, own, across, *rest):
    along, rows = rest[:4], rest[4]
    slot = pl.program_id(0) // 2
    v_high, v_low = split(volume[...].reshape(1024, 256))
    rows[...] = dot3(high[...], low[...], v_high, v_low)

    def block(part, q):
        begin = places[B_SETS + slot * 8 + part * 2 + q] * 128
        return rows[pl.ds(pl.multiple_of(begin, 128), 128), :]

    for q in range(2):
        own[0, q, 0] = block(0, q)
        across[0, q, 0] = block(1, q)
        for side in range(2):

            @pl.when(slot == side)
            def _():
                along[2 * side][q, 0] = block(2, q)
                along[2 * side + 1][q, 0] = block(3, q)


def y_forward(places, volume, high, low):
    whole = pl.BlockSpec((1024, 1024), lambda c: (0, 0))
    both = pl.BlockSpec((1, 2, 1, 128, 256), lambda c: (c // 2, 0, c % 2, 0, 0))
    down = pl.BlockSpec((2, 1, 128, 256), lambda c: (0, jnp.minimum(c, 1), 0, 0))
    up = pl.BlockSpec((2, 1, 128, 256), lambda c: (0, jnp.maximum(c - 2, 0), 0, 0))
    return pl.pallas_call(
        y_forward_kernel,
        grid=(4,),
        in_specs=[SMEM, pl.BlockSpec((32, 1, 32, 256), lambda c: (0, c, 0, 0)), whole, whole],
        out_specs=[both, both, down, down, up, up],
        out_shape=[BOTH, BOTH] + [PART] * 4,
        scratch_shapes=[pltpu.VMEM((1024, 256), F32)],
        compiler_params=pltpu.CompilerParams(vmem_limit_bytes=EDGE_LIMIT),
        cost_estimate=cost(6 * 2**30, 12),
        name="y_forward",
    )(places, volume, high, low)


def x_forward_kernel(places, own, across, *refs):
    along, (high, low, out, v_high, v_low) = refs[:4], refs[4:]
    step = pl.program_id(0)

    @pl.when(step == 0)
    def _():
        for slot in range(2):
            for k in range(4):
                part = (own, across)[k].at[slot] if k < 2 else along[2 * slot + k - 2]
                rows = pl.ds(slot * 512, 512)
                lanes = pl.ds(pl.multiple_of(places[X_BLOCKS + k] * 256, 256), 256)
                v_high[rows, lanes], v_low[rows, lanes] = split(part[...].reshape(512, 256))

    total = dot3(v_high[...], v_low[...], high[...], low[...])
    out[...] = total.reshape(2, 2, 2, 128, 256)


def x_forward(places, own, across, along, high, low):
    return pl.pallas_call(
        x_forward_kernel,
        grid=(4,),
        in_specs=[SMEM]
        + [pl.BlockSpec((2, 2, 2, 128, 256), lambda a: (0, 0, 0, 0, 0))] * 2
        + [pl.BlockSpec((2, 2, 128, 256), lambda a: (0, 0, 0, 0))] * 4
        + [pl.BlockSpec((1024, 256), lambda a: (0, a))] * 2,
        out_specs=pl.BlockSpec((2, 2, 2, 128, 256), lambda a: (0, 0, 0, 0, a)),
        out_shape=jax.ShapeDtypeStruct((2, 2, 2, 128, 1024), F32),
        scratch_shapes=[pltpu.VMEM((1024, 1024), BF16)] * 2,
        compiler_params=pltpu.CompilerParams(vmem_limit_bytes=EDGE_LIMIT),
        cost_estimate=cost(6 * 2**30, 12),
        name="x_forward",
    )(places, own, across, *along, high, low)


def x_inverse_kernel(_, spectrum, near, above, below, high, low, own, across, *rest):
    along, (v_high, v_low) = rest[:4], rest[4:]
    step = pl.program_id(0)

    @pl.when(step == 0)
    def _():
        for slot in range(2):
            for q in range(2):
                for c in range(2):
                    psf = (above, below)[slot][:, c] if q else near[:, slot, c]
                    value = spectrum[slot, q, c] * psf.reshape(128, 1024)
                    rows = pl.ds(slot * 512 + q * 256 + c * 128, 128)
                    v_high[rows, :], v_low[rows, :] = split(value)

    result = dot3(v_high[...], v_low[...], high[0], low[0]).reshape(2, 2, 2, 128, 256)
    for k in range(2):

        @pl.when(step == k)
        def _():
            along[k][...] = result[0]
            along[2 + k][...] = result[1]

    @pl.when(step == 2)
    def _():
        across[...] = result

    @pl.when(step == 3)
    def _():
        own[...] = result


def x_inverse(places, spectrum, near, above, below, high, low):
    def block(step, places):
        return places[X_BLOCKS + jnp.where(step < 2, step + 2, 3 - step)], 0, 0

    table = pl.BlockSpec((1, 1024, 256), block)
    whole = pl.BlockSpec((2, 2, 2, 128, 1024), lambda step, places: (0, 0, 0, 0, 0))
    far = pl.BlockSpec((16, 2, 8, 1024), lambda step, places: (0, 0, 0, 0))
    return pl.pallas_call(
        x_inverse_kernel,
        grid_spec=pltpu.PrefetchScalarGridSpec(
            num_scalar_prefetch=1,
            grid=(4,),
            in_specs=[whole, VMEM, far, far, table, table],
            out_specs=[VMEM] * 6,
            scratch_shapes=[pltpu.VMEM((1024, 1024), BF16)] * 2,
        ),
        out_shape=[BOTH, BOTH] + [PART] * 4,
        compiler_params=pltpu.CompilerParams(vmem_limit_bytes=X_LIMIT),
        cost_estimate=cost(6 * 2**30, 16),
        name="x_inverse",
    )(places, spectrum, near, above, below, high, low)


def y_inverse_kernel(places, own, across, *refs):
    along, (high, low, out, v_high, v_low) = refs[:4], refs[4:]
    slot, c = pl.program_id(0) // 2, pl.program_id(0) % 2

    def place(part, q, value):
        begin = places[B_SETS + slot * 8 + part * 2 + q] * 128
        rows = pl.ds(pl.multiple_of(begin, 128), 128)
        v_high[rows, :], v_low[rows, :] = split(value)

    for q in range(2):
        place(0, q, own[slot, q, c])
        place(1, q, across[slot, q, c])
        for side in range(2):

            @pl.when(slot == side)
            def _():
                place(2, q, along[2 * side][q, c])
                place(3, q, along[2 * side + 1][q, c])

    result = dot3(high[...], low[...], v_high[...], v_low[...])
    out[:, 2 * slot + c] = result.reshape(32, 32, 256)


def y_inverse(places, own, across, along, high, low):
    return pl.pallas_call(
        y_inverse_kernel,
        grid=(4,),
        in_specs=[SMEM] + [VMEM] * 8,
        out_specs=VMEM,
        out_shape=jax.ShapeDtypeStruct((32, 4, 32, 256), F32),
        scratch_shapes=[pltpu.VMEM((1024, 256), BF16)] * 2,
        compiler_params=pltpu.CompilerParams(vmem_limit_bytes=LIMIT),
        cost_estimate=cost(6 * 2**30, 12),
        name="y_inverse",
    )(places, own, across, *along, high, low)


def local(ratio_field, estimate, psf_spectrum):
    px, zh, py, zl, core = (lax.axis_index(name) for name in ALL)
    ring = 2 * zh + zl
    narrow = 2 * zl + core

    cz = cosine_table(128)
    cz_order = np.array(
        [
            [
                (gx * 4 + gy) * 8 + ((2 * h + low - 1 + side) % 4) * 2 + i
                for gx in range(4)
                for h in range(2)
                for gy in range(4)
                for side in range(2)
                for i in range(2)
            ]
            for low in range(2)
        ]
    )
    z_rows = [jnp.asarray(h) for h in halves(cz[cz_order])]
    pick_order = np.array(
        [
            [
                g * 8 + ((r + shift) % 4) * 2 + i
                for shift in (-1, 0, -2, 1)
                for g in range(16)
                for i in range(2)
            ]
            for r in range(4)
        ]
    )
    pick = jnp.asarray(np.eye(128, dtype=np.float32)[pick_order].astype(ml_dtypes.bfloat16))
    cy = cosine_table(1024)
    b_order = np.array(
        [
            (((gx * 2 + r // 2) * 4 + gy) * 2 + r % 2) * 16 + k * 8 + j
            for r in range(4)
            for k in range(2)
            for gx in range(4)
            for gy in range(4)
            for j in range(8)
        ]
    )
    y_rows = [jnp.asarray(h) for h in halves(cy[b_order])]
    y_columns = [jnp.asarray(h) for h in halves(np.ascontiguousarray(cy[b_order].T))]
    cx = cosine_table(1024)
    x_rows = [jnp.asarray(h) for h in halves(np.ascontiguousarray(cx.T))]
    x_columns = [
        jnp.asarray(h) for h in halves(np.ascontiguousarray(cx.reshape(1024, 4, 256).transpose(1, 0, 2)))
    ]

    partners = ((0, 0), (0, 1), (1, 0), (1, 1))
    places = [ring] + [narrow ^ (2 * far + flip) for far, flip in partners]
    for sign in (-1, 1):
        for far, flip in partners:
            for q in range(2):
                place = ring + sign * (1 + q) if far else ring - sign * q
                places.append((place % 4) * 2 + (core ^ flip))
    places = jnp.stack(places).astype(jnp.int32)

    def send(value, step, flip):
        return lax.ppermute(value, ALL, moves(step, flip))

    def first_all_to_all(value, axes):
        return lax.all_to_all(value, axes, split_axis=0, concat_axis=0, tiled=True)

    def one(value):
        return jnp.asarray(value, jnp.int32).reshape(1)

    def after(value, done):
        return lax.optimization_barrier((value, done))[0]

    volume = z_forward(one(zl), ratio_field, *z_rows)
    volume = first_all_to_all(volume, ("x", "zh", "y")).reshape(32, 4, 32, 256)

    near, far = psf_forward(places, psf_spectrum, pick)
    far = first_all_to_all(after(far, volume), ("x", "y"))

    def exchange(own, across, *along):
        from_above = [send(along[0], -1, 0), send(along[1], -1, 1)]
        from_below = [send(along[2], 1, 0), send(along[3], 1, 1)]
        return own, send(across, 0, 1), from_below + from_above

    parts = exchange(*y_forward(places, volume, *y_rows))
    near = first_all_to_all(after(near, (far, parts[1], parts[2][0], parts[2][2])), ("x", "y"))
    above, below = send(far[:, 0], -1, 0), send(far[:, 1], 1, 0)
    spectrum = x_forward(places, *parts, *x_rows)
    parts = exchange(*x_inverse(places, spectrum, near, above, below, *x_columns))
    volume = y_inverse(places, *parts, *y_columns)

    volume = first_all_to_all(volume.reshape(128, 32, 256), ("x", "zh", "y"))
    return z_inverse(one(zl), volume, estimate, *z_rows)


def solution(mesh):
    cut = jax.sharding.Mesh(mesh.devices.reshape(4, 2, 4, 2, 2), ALL)
    wide, narrow = ("x", "zh", "y"), ("zl", "core")
    placed = (P(narrow, wide, None), P(narrow, wide, None), P(None, wide + narrow, None))
    return jax.shard_map(
        local, mesh=cut, in_specs=placed, out_specs=P(narrow, wide, None), check_vma=False
    )
```
